32 devices in a mesh: seq: 16 (over z, y, x), head: 2 (over core).
Axes of the slice: x: 2, y: 2, z: 4, core: 2. Of those that a mesh axis runs over, the one named last changes fastest.
Arguments:
- queries: bfloat16 [6144, 1536], P('seq', 'head'), may hold values from -100 to 100
- keys: bfloat16 [6144, 1536], P('seq', 'head'), may hold values from -5 to 5
- values: bfloat16 [6144, 1536], P('seq', 'head'), may hold values from -6 to 6
- membership: int32 [12, 6144, 1], P('head', 'seq'), may hold values from 0 to 63, as said below
- w_out: bfloat16 [1536, 1536], P('head'), may hold values from -0.15625 to 0.15625
Outputs:
- projected: bfloat16 [6144, 1536], P('seq', 'head')
The draws below stay inside these ranges and needn't reach their ends.
Inputs may be any that keep to these rules, and one draw needn't show every extreme that they name: `membership`: among the 384 tokens of one index of seq, in one head, no cluster holds more than 12 tokens, and some cluster holds exactly 12.
All inputs are finite; a program needn't handle non-finite values.
Results may differ from the reference program's by a relative error of at most 0.0056.
Values may be sent and summed in bfloat16 or wider, within the bound.
No kernel may reach another device: no remote copies, remote signals or barrier semaphores. Data moves between devices by JAX's collectives and lax.ppermute only.
A program may use at most 64 MiB of HBM per device.

```python
import math
import jax
import jax.numpy as jnp
from jax import lax

D = 1536
HEADS = 12
HD = 128
TOK_DEV = 384
TOKENS = 6144
CLUSTERS = 64
CAP = 12
N_SEQ = 16


def member_table(key):
    device_count = TOKENS // TOK_DEV
    groups = (TOK_DEV + CAP - 1) // CAP
    popular = (jax.random.randint(jax.random.fold_in(key, 7101), (HEADS, 1, CLUSTERS), 0, 8) == 0).astype(jnp.int32)
    score = jax.random.randint(jax.random.fold_in(key, 7102), (HEADS, device_count, CLUSTERS), 0, CLUSTERS)
    score = score + popular * (CLUSTERS // 2)
    distinct = score * CLUSTERS + jnp.arange(CLUSTERS, dtype=jnp.int32)[None, None, :]
    picked_scores, chosen = lax.top_k(distinct, groups)
    order_key = jax.random.randint(jax.random.fold_in(key, 7103), (HEADS, device_count, TOK_DEV), 0, TOK_DEV)
    order_key = order_key * TOK_DEV + jnp.arange(TOK_DEV, dtype=jnp.int32)[None, None, :]
    shuffle = jnp.argsort(order_key, axis=-1, stable=True).astype(jnp.int32)
    group_of = shuffle // CAP
    cluster = jnp.take_along_axis(chosen.astype(jnp.int32), group_of, axis=-1)
    return cluster.reshape(HEADS, TOKENS).astype(jnp.int32)


def center_rows(key):
    member = member_table(key)
    centers = jax.random.normal(jax.random.fold_in(key, 7201), (HEADS, CLUSTERS, HD), jnp.float32)
    rows = jnp.take_along_axis(centers, member[:, :, None], axis=1)
    return rows.transpose(1, 0, 2).reshape(TOKENS, D)


def base_keys(key):
    noise = jax.random.normal(jax.random.fold_in(key, 7001), (TOKENS, D), jnp.float32)
    return jnp.clip(0.8 * center_rows(key) + 0.6 * noise, -5.0, 5.0)


def draw_membership(key, part):
    return member_table(key)[:, :, None]


def draw_keys(key, part):
    return base_keys(key).astype(jnp.bfloat16)


def draw_queries(key, part):
    centers = center_rows(key)
    noise = jax.random.normal(jax.random.fold_in(key, 7002), (TOKENS, D), jnp.float32)
    fresh = jnp.clip(0.8 * centers + 0.6 * noise, -5.0, 5.0)
    return fresh.astype(jnp.bfloat16)


def block_scale(own_key, shape, cuts, smallest, high):
    gain, own = 1.0, jax.random.fold_in(own_key, 6)
    for dim, parts in cuts:
        heights = jnp.exp(jax.random.uniform(jax.random.fold_in(own, dim), (parts,), jnp.float32, smallest / len(cuts), high / len(cuts)))
        gain = gain * jnp.repeat(heights, shape[dim] // parts).reshape([-1 if axis == dim else 1 for axis in range(len(shape))])
    return gain


def scatter_about(rng, dims, scale, bound, pieces=(), kind=jnp.bfloat16):
    loudness = block_scale(rng, dims, pieces, -0.22, 0.18) if pieces else 1.0
    result = jax.random.normal(rng, dims, jnp.float32) * scale * loudness
    return jnp.minimum(jnp.maximum(result, -bound), bound).astype(kind)


def setup_inputs(seed: int = 0) -> dict:
    seeds = jax.random.split(jax.random.key(seed), 6)
    queries = draw_queries(jax.random.fold_in(seeds[5], 71), 0)
    keys = draw_keys(jax.random.fold_in(seeds[5], 71), 0)
    values = scatter_about(seeds[2], (TOKENS, D), 1.0, 6.0, ((0, 16), (1, 2)))
    membership = draw_membership(jax.random.fold_in(seeds[5], 71), 0)
    w_out = scatter_about(seeds[4], (D, D), D ** -0.5, 0.15625, ((0, 2),))
    return dict(queries=queries, keys=keys, values=values, membership=membership, w_out=w_out)


NEG = -1e+30

def attend(block, live, own, centers, counts):
    scale = 1.0 / math.sqrt(HD)
    query = block[..., :HD].astype(jnp.float32)
    key_rows = block[..., HD:2 * HD].astype(jnp.float32)
    value_rows = block[..., 2 * HD:].astype(jnp.float32)
    exact = jnp.einsum('gqd,gkd->gqk', query, key_rows) * scale
    exact = jnp.where(live[:, None, :] > 0, exact, NEG)
    mean_keys = centers[:, :HD].astype(jnp.float32)
    mean_values = centers[:, HD:].astype(jnp.float32)
    weights = jnp.log(jnp.maximum(counts, 1.0))
    far_scores = jnp.einsum('gqd,cd->gqc', query, mean_keys) * scale + weights[None, None, :]
    labels = jnp.arange(counts.shape[0], dtype=jnp.int32)
    valid = (counts[None, :] > 0) & (labels[None, :] != own[:, None])
    far_scores = jnp.where(valid[:, None, :], far_scores, NEG)
    top = jnp.maximum(lax.optimization_barrier(jnp.max(exact, -1)), lax.optimization_barrier(jnp.max(far_scores, -1)))
    near = jnp.exp(exact - top[..., None])
    far = jnp.exp(far_scores - top[..., None])
    total = lax.optimization_barrier(jnp.sum(near, -1)) + lax.optimization_barrier(jnp.sum(far, -1))
    near_b = near.astype(jnp.bfloat16).astype(jnp.float32)
    far_b = far.astype(jnp.bfloat16).astype(jnp.float32)
    mixed = jnp.einsum('gqk,gkd->gqd', near_b, value_rows) + jnp.einsum('gqc,cd->gqd', far_b, mean_values)
    return (mixed / total[..., None]).astype(jnp.bfloat16)

def reference(queries, keys, values, membership, w_out):
    labels = jnp.arange(CLUSTERS, dtype=jnp.int32)
    owner_slots = N_SEQ * CAP
    group = math.gcd(CLUSTERS, 16)

    def one_head(h):
        start = (h * HD).astype(jnp.int32)
        q = lax.dynamic_slice_in_dim(queries, start, HD, 1)
        k = lax.dynamic_slice_in_dim(keys, start, HD, 1)
        v = lax.dynamic_slice_in_dim(values, start, HD, 1)
        member = lax.dynamic_index_in_dim(membership, h, 0, keepdims=False)[:, 0].astype(jnp.int32)
        onehot = (member[:, None] == labels[None, :]).astype(jnp.int32).reshape(N_SEQ, TOK_DEV, CLUSTERS)
        before = (jnp.cumsum(onehot, axis=1) - onehot).astype(jnp.int32)
        slot = lax.optimization_barrier(jnp.sum(before * onehot, axis=2)).astype(jnp.int32).reshape(TOKENS)
        device = jnp.arange(TOKENS, dtype=jnp.int32) // TOK_DEV
        position = (device * CAP + slot).astype(jnp.int32)
        rows = jnp.concatenate([q, k, v], 1)
        tiles = jnp.zeros((CLUSTERS, owner_slots, 3 * HD), jnp.bfloat16).at[member, position].set(rows)
        live = jnp.zeros((CLUSTERS, owner_slots), jnp.float32).at[member, position].set(1.0)
        pairs = jnp.concatenate([k, v], 1).astype(jnp.float32)
        sums = jax.ops.segment_sum(pairs, member, num_segments=CLUSTERS)
        counts = jax.ops.segment_sum(jnp.ones((TOKENS,), jnp.float32), member, num_segments=CLUSTERS)
        centers = (sums / jnp.maximum(counts, 1.0)[:, None]).astype(jnp.bfloat16)

        def one_group(g):
            first = (g * group).astype(jnp.int32)
            block = lax.dynamic_slice_in_dim(tiles, first, group, 0)
            block_live = lax.dynamic_slice_in_dim(live, first, group, 0)
            own = first + jnp.arange(group, dtype=jnp.int32)
            return attend(block, block_live, own, centers, counts)
        answers = lax.map(one_group, jnp.arange(CLUSTERS // group, dtype=jnp.int32))
        answers = answers.reshape(CLUSTERS, owner_slots, HD)
        return answers[member, position]
    heads_out = lax.map(one_head, jnp.arange(HEADS, dtype=jnp.int32))
    attended = heads_out.transpose(1, 0, 2).reshape(TOKENS, D)
    return jnp.dot(attended, w_out, preferred_element_type=jnp.float32).astype(jnp.bfloat16)
```

```python
import functools
import math

import jax
import jax.numpy as jnp
from jax import lax
from jax.experimental import pallas as pl
from jax.experimental.pallas import tpu as pltpu
from jax.sharding import PartitionSpec as P

CL_DEV = 4
NEG = -1e30
EMPTY = 128.0
VMEM_LIMIT = 56 * 1024 * 1024


def iota(shape, dim):
    return lax.broadcasted_iota(jnp.int32, shape, dim)


def nt_dot(a, b):
    return lax.dot_general(a, b, (((1,), (1,)), ((), ())), preferred_element_type=jnp.float32)


def nn_dot(a, b):
    return jnp.dot(a, b, preferred_element_type=jnp.float32)


def pack_kernel(rows, cap, row_ref, col_ref, q_ref, k_ref, v_ref, send_ref, place_ref):
    tok, hd = q_ref.shape
    n_seq = send_ref.shape[0]
    slots = n_seq * rows
    member = row_ref[0]
    column = col_ref[0]
    t_first, t_second = iota((tok, tok), 0), iota((tok, tok), 1)
    same = column == member
    earlier = jnp.where(same & (t_first < t_second), 1.0, 0.0)
    slot = jnp.sum(earlier, axis=0, keepdims=True).astype(jnp.int32)
    place = (member // CL_DEV) * rows + (member % CL_DEV) * cap + slot
    later = jnp.where(same & (t_second < t_first), 1.0, 0.0)
    slot_col = jnp.sum(later, axis=1, keepdims=True).astype(jnp.int32)
    place_ref[0] = (column // CL_DEV) * rows + (column % CL_DEV) * cap + slot_col
    hot = jnp.where(iota((slots, tok), 0) == place, 1.0, 0.0).astype(jnp.bfloat16)
    ones = jnp.ones((tok, hd), jnp.bfloat16)
    packed_kv = nn_dot(hot, jnp.concatenate([k_ref[...], v_ref[...]], 1))
    packed_q = nn_dot(hot, jnp.concatenate([q_ref[...], ones], 1))
    live = packed_q[:, hd:]
    mark = jnp.where(iota((slots, hd), 1) == 0, EMPTY, 0.0)
    key = packed_kv[:, :hd] + mark * (1.0 - live)
    send_ref[:, 0, :, :hd] = packed_q[:, :hd].astype(jnp.bfloat16).reshape(n_seq, rows, hd)
    send_ref[:, 0, :, hd : 2 * hd] = key.astype(jnp.bfloat16).reshape(n_seq, rows, hd)
    send_ref[:, 0, :, 2 * hd :] = packed_kv[:, hd:].astype(jnp.bfloat16).reshape(n_seq, rows, hd)


def local_cluster(index, rows, cap):
    return lax.rem(index, rows) // cap


def live_row(key):
    hd = key.shape[1]
    pick = jnp.where(iota((16, hd), 1) == 0, 1.0, 0.0).astype(jnp.bfloat16)
    first = nt_dot(pick, key)
    return jnp.where(first < 0.5 * EMPTY, 1.0, 0.0)


def centers_kernel(rows, cap, recv_ref, out_ref, acc_ref, count_ref):
    h = pl.program_id(0)
    heads = pl.num_programs(0)
    n_seq = recv_ref.shape[0]
    slots = n_seq * rows
    hd = recv_ref.shape[3] // 3
    total_rows = out_ref.shape[1]

    @pl.when(h == 0)
    def _():
        acc_ref[...] = jnp.zeros_like(acc_ref)
        count_ref[...] = jnp.zeros_like(count_ref)

    key = recv_ref[:, 0, :, hd : 2 * hd].reshape(slots, hd)
    pairs = recv_ref[:, 0, :, hd:].reshape(slots, 2 * hd)
    live = live_row(key)
    line = iota((total_rows, slots), 0) - h * CL_DEV
    cluster = local_cluster(iota((total_rows, slots), 1), rows, cap)
    chosen = jnp.where((line == cluster) & (live[:1] > 0), 1.0, 0.0)
    acc_ref[...] += nn_dot(chosen.astype(jnp.bfloat16), pairs)
    count_ref[...] += jnp.sum(chosen, axis=1, keepdims=True)

    @pl.when(h == heads - 1)
    def _():
        count = count_ref[...]
        centers = acc_ref[...] / jnp.maximum(count, 1.0)
        r, l = iota(acc_ref.shape, 0), iota(acc_ref.shape, 1)
        diagonal = jnp.sum(jnp.where(r == l, count, 0.0), axis=0, keepdims=True)
        block = jnp.where(r == heads * CL_DEV, diagonal, centers).astype(jnp.bfloat16)
        for j in range(n_seq):
            out_ref[j] = block


def attend_kernel(rows, cap, step, rank_ref, all_ref, recv_ref, out_ref, cent_ref, bias_ref, dead_ref):
    h = pl.program_id(0)
    heads = pl.num_programs(0)
    n_seq = recv_ref.shape[0]
    slots = n_seq * rows
    hd = recv_ref.shape[3] // 3
    clusters = n_seq * CL_DEV
    block = all_ref.shape[1]
    far = cent_ref.shape[1]
    root = math.sqrt(hd)

    @pl.when(h == 0)
    def _():
        everything = all_ref[...].reshape(n_seq * block, 2 * hd)
        r = iota((far, n_seq * block), 1)
        c = iota((far, n_seq * block), 0)
        inside = c < clusters
        last = (c // CL_DEV) * block + heads * CL_DEV
        tall = jnp.where((r == last) & inside, 1.0, 0.0).astype(jnp.bfloat16)
        counts = nn_dot(tall, everything)
        lane, line = iota((far, 2 * hd), 1), iota((far, 2 * hd), 0)
        ones = jnp.ones((16, 2 * hd), jnp.bfloat16)
        for i in range(heads_of(cent_ref)):
            base = (c // CL_DEV) * block + i * CL_DEV + lax.rem(c, CL_DEV)
            hot = jnp.where((r == base) & inside, 1.0, 0.0).astype(jnp.bfloat16)
            cent_ref[i] = nn_dot(hot, everything).astype(jnp.bfloat16)
            mine = jnp.where(lane == i * CL_DEV + lax.rem(line, CL_DEV), counts, 0.0)
            row = nt_dot(ones, mine.astype(jnp.bfloat16))[:8]
            bias_ref[i] = jnp.log(jnp.maximum(row, 1.0)) * root
            dead_ref[i] = jnp.broadcast_to(jnp.sum(mine, axis=1, keepdims=True), (far, hd))

    rank = rank_ref[0]
    key = recv_ref[:, 0, :, hd : 2 * hd].reshape(slots, hd)
    value = recv_ref[:, 0, :, 2 * hd :].reshape(slots, hd)
    query = recv_ref[:, 0, :, :hd].reshape(slots, hd)
    lane = iota((slots, hd), 1)
    cluster = local_cluster(iota((slots, hd), 0), rows, cap)
    query_side = jnp.where(lane == cluster, 1.0, 0.0).astype(jnp.bfloat16)
    empty = key[:, :1].astype(jnp.float32) > 0.5 * EMPTY
    key_side = jnp.where((lane == cluster) & jnp.logical_not(empty), 0.0, NEG).astype(jnp.bfloat16)
    far_lane, far_line = iota((far, hd), 1), iota((far, hd), 0)
    own = far_lane + rank * CL_DEV == far_line
    far_side = jnp.where((dead_ref[h] > 0) & jnp.logical_not(own), 0.0, NEG).astype(jnp.bfloat16)
    near_keys = jnp.concatenate([key, key_side], 1)
    centers = cent_ref[h]
    far_keys = jnp.concatenate([centers[:, :hd], far_side], 1)
    near_values = jnp.concatenate([value, jnp.ones((slots, hd), jnp.bfloat16)], 1)
    far_values = jnp.concatenate([centers[:, hd:], jnp.ones((far, hd), jnp.bfloat16)], 1)
    queries = jnp.concatenate([query, query_side], 1)
    scale = math.log2(math.e) / root
    for start in range(0, slots, step):
        q = queries[start : start + step]
        near = nt_dot(q, near_keys)
        distant = nt_dot(q, far_keys) + bias_ref[h][:1]
        top = jnp.maximum(jnp.max(near, 1, keepdims=True), jnp.max(distant, 1, keepdims=True))
        near = jnp.exp2((near - top) * scale).astype(jnp.bfloat16)
        distant = jnp.exp2((distant - top) * scale).astype(jnp.bfloat16)
        mixed = nn_dot(near, near_values) + nn_dot(distant, far_values)
        answer = (mixed[:, :hd] / mixed[:, hd:]).astype(jnp.bfloat16)
        first = start // rows
        out_ref[first : first + step // rows, 0] = answer.reshape(step // rows, rows, hd)


def heads_of(ref):
    return ref.shape[0]


def unpack_kernel(place_ref, back_ref, out_ref):
    n_seq, _, rows, hd = back_ref.shape
    tok = out_ref.shape[0]
    slots = n_seq * rows
    hot = jnp.where(iota((tok, slots), 1) == place_ref[0], 1.0, 0.0).astype(jnp.bfloat16)
    out_ref[...] = nn_dot(hot, back_ref[:, 0].reshape(slots, hd)).astype(jnp.bfloat16)


def per_device(queries, keys, values, membership, w_out):
    n_seq = lax.axis_size("seq")
    groups = lax.axis_size("head")
    rank = lax.axis_index("seq")
    group = lax.axis_index("head")
    tok = queries.shape[0]
    heads = membership.shape[0]
    hd = queries.shape[1] // heads
    width = w_out.shape[1] // groups
    clusters = CL_DEV * n_seq
    cap = max(2, (2 * tok + clusters - 1) // clusters)
    rows = (CL_DEV * cap + 15) // 16 * 16
    slots = n_seq * rows
    params = pltpu.CompilerParams(
        dimension_semantics=("arbitrary",), vmem_limit_bytes=VMEM_LIMIT
    )
    exchange = functools.partial(
        lax.all_to_all, axis_name="seq", split_axis=0, concat_axis=0, tiled=True
    )
    swap = [(i, (i + 1) % groups) for i in range(groups)]

    mine = lax.dynamic_slice_in_dim(w_out, group * width, width, 1)
    other = lax.dynamic_slice_in_dim(w_out, (1 - group) * width, width, 1)
    other = lax.ppermute(other, "head", swap)

    matrix = pl.BlockSpec((tok, hd), lambda h: (0, h))
    line = pl.BlockSpec((1, 1, tok), lambda h: (h, 0, 0))
    column = pl.BlockSpec((1, tok, 1), lambda h: (h, 0, 0))

    def slot_block(depth):
        return pl.BlockSpec((n_seq, 1, rows, depth), lambda h: (0, h, 0, 0))

    send, place = pl.pallas_call(
        functools.partial(pack_kernel, rows, cap),
        grid=(heads,),
        in_specs=[line, column, matrix, matrix, matrix],
        out_specs=[slot_block(3 * hd), column],
        out_shape=[
            jax.ShapeDtypeStruct((n_seq, heads, rows, 3 * hd), jnp.bfloat16),
            jax.ShapeDtypeStruct((heads, tok, 1), jnp.int32),
        ],
        compiler_params=params,
        name="pack",
    )(membership.reshape(heads, 1, tok), membership, queries, keys, values)
    received = exchange(send)

    center_rows = (heads * CL_DEV + 1 + 15) // 16 * 16
    centers = pl.pallas_call(
        functools.partial(centers_kernel, rows, cap),
        grid=(heads,),
        in_specs=[slot_block(3 * hd)],
        out_specs=pl.BlockSpec((n_seq, center_rows, 2 * hd), lambda h: (0, 0, 0)),
        out_shape=jax.ShapeDtypeStruct((n_seq, center_rows, 2 * hd), jnp.bfloat16),
        scratch_shapes=[
            pltpu.VMEM((center_rows, 2 * hd), jnp.float32),
            pltpu.VMEM((center_rows, 1), jnp.float32),
        ],
        compiler_params=params,
        name="centers",
    )(received)
    all_centers = exchange(centers)

    far = (clusters + 127) // 128 * 128
    step = rows
    while step * 2 <= 384 and slots % (step * 2) == 0:
        step *= 2
    answers = pl.pallas_call(
        functools.partial(attend_kernel, rows, cap, step),
        grid=(heads,),
        in_specs=[
            pl.BlockSpec(memory_space=pltpu.SMEM),
            pl.BlockSpec((n_seq, center_rows, 2 * hd), lambda h: (0, 0, 0)),
            slot_block(3 * hd),
        ],
        out_specs=slot_block(hd),
        out_shape=jax.ShapeDtypeStruct((n_seq, heads, rows, hd), jnp.bfloat16),
        scratch_shapes=[
            pltpu.VMEM((heads, far, 2 * hd), jnp.bfloat16),
            pltpu.VMEM((heads, 8, far), jnp.float32),
            pltpu.VMEM((heads, far, hd), jnp.float32),
        ],
        compiler_params=params,
        name="attend",
    )(rank.reshape(1), all_centers, received)
    returned = exchange(answers)

    attended = pl.pallas_call(
        unpack_kernel,
        grid=(heads,),
        in_specs=[column, slot_block(hd)],
        out_specs=matrix,
        out_shape=jax.ShapeDtypeStruct((tok, heads * hd), jnp.bfloat16),
        compiler_params=params,
        name="unpack",
    )(place, returned)
    partner = lax.ppermute(attended, "head", swap)
    result = nn_dot(attended, mine) + nn_dot(partner, other)
    return result.astype(jnp.bfloat16)


def solution(mesh):
    return jax.shard_map(
        per_device,
        mesh=mesh,
        in_specs=(
            P("seq", "head"),
            P("seq", "head"),
            P("seq", "head"),
            P("head", "seq", None),
            P("head", None),
        ),
        out_specs=P("seq", "head"),
        check_vma=False,
    )
```

```python
import functools
import math

import jax
import jax.numpy as jnp
from jax import lax
from jax.experimental import pallas as pl
from jax.experimental.pallas import tpu as pltpu
from jax.sharding import PartitionSpec as P

CL_DEV = 4
NEG = -1e30
EMPTY = 128.0
BF16 = jnp.bfloat16
F32 = jnp.float32


def iota(shape, dim):
    return lax.broadcasted_iota(jnp.int32, shape, dim)


def nt_dot(a, b):
    return lax.dot_general(a, b, (((1,), (1,)), ((), ())), preferred_element_type=F32)


def nn_dot(a, b):
    return jnp.dot(a, b, preferred_element_type=F32)


def one_zero(mask, kind=BF16):
    return jnp.where(mask, 1.0, 0.0).astype(kind)


def pack_kv_kernel(rows, cap, member_ref, k_ref, v_ref, send_ref, place_ref, lower_ref):
    tok = k_ref.shape[0]
    n_seq, per_step = send_ref.shape[:2]
    hd = k_ref.shape[1] // per_step
    slots = n_seq * rows
    clusters = n_seq * CL_DEV

    @pl.when(pl.program_id(0) == 0)
    def _():
        lower_ref[...] = one_zero(iota((tok, tok), 0) < iota((tok, tok), 1))

    for i in range(per_step):
        member = member_ref[i]
        same = iota((clusters, tok), 0) == member
        before = nn_dot(one_zero(same), lower_ref[...])
        slot = jnp.sum(jnp.where(same, before, 0.0), axis=0, keepdims=True).astype(jnp.int32)
        place = (member // CL_DEV) * rows + (member % CL_DEV) * cap + slot
        place_ref[i] = place
        hot = one_zero(iota((slots, tok), 0) == place, F32)
        live = jnp.sum(hot, axis=1, keepdims=True)
        span = slice(i * hd, (i + 1) * hd)
        pair = jnp.concatenate([k_ref[:, span], v_ref[:, span]], 1)
        packed = nn_dot(hot.astype(BF16), pair)
        mark = jnp.where(iota((slots, 2 * hd), 1) == 0, EMPTY * (1.0 - live), 0.0)
        send_ref[:, i] = (packed + mark).astype(BF16).reshape(n_seq, rows, 2 * hd)


def pack_q_kernel(rows, place_ref, q_ref, send_ref, column_ref):
    tok = q_ref.shape[0]
    n_seq = send_ref.shape[0]
    per_step = send_ref.shape[1] // rows
    hd = q_ref.shape[1] // per_step
    slots = n_seq * rows
    h = pl.program_id(0) * per_step

    @pl.when(h == 0)
    def _():
        column_ref[...] = jnp.zeros_like(column_ref)

    for i in range(per_step):
        place = place_ref[i]
        hot = one_zero(iota((slots, tok), 0) == place)
        packed = nn_dot(hot, q_ref[:, i * hd : (i + 1) * hd])
        send_ref[:, i * rows : (i + 1) * rows] = packed.astype(BF16).reshape(n_seq, rows, hd)
        turned = jnp.broadcast_to(place.astype(F32), (128, tok)).T.astype(jnp.int32)
        column_ref[...] += jnp.where(iota((tok, 128), 1) == h + i, turned, 0)


def regroup_kernel(rows, cap, recv_ref, key_ref, value_ref, perm_ref):
    h = pl.program_id(0)
    n_seq = recv_ref.shape[0]
    slots = n_seq * rows
    near = n_seq * cap
    hd = recv_ref.shape[3] // 2

    @pl.when(h == 0)
    def _():
        line = iota((near, 1), 0)
        source = line // cap
        origin = source * rows + (line - source * cap)
        for e in range(CL_DEV):
            perm_ref[e] = one_zero(iota((near, slots), 1) == origin + e * cap)

    pairs = recv_ref[:, 0].reshape(slots, 2 * hd)
    lane = iota((near, hd), 1)
    for e in range(CL_DEV):
        grouped = nn_dot(perm_ref[e], pairs)
        live = grouped[:, :1] < 0.5 * EMPTY
        kept = jnp.where(live, grouped, 0.0).astype(BF16)
        key_ref[0, e, :, :hd] = kept[:, :hd]
        key_ref[0, e, :, hd:] = jnp.where((lane == 0) & jnp.logical_not(live), NEG, 0.0).astype(BF16)
        value_ref[0, e, :, :hd] = kept[:, hd:]
        value_ref[0, e, :, hd:] = jnp.ones((near, hd), BF16)


def centers_kernel(cap, heads, recv_ref, buffer_ref, send_ref, acc_ref, count_ref, block_ref, sem):
    del buffer_ref
    n_seq, per_step, rows, _ = recv_ref.shape
    extra, hd = acc_ref.shape
    owned = heads * CL_DEV
    step = pl.program_id(0)

    @pl.when(step == 0)
    def _():
        acc_ref[...] = jnp.zeros_like(acc_ref)
        count_ref[...] = jnp.zeros_like(count_ref)

    line = iota((extra, 1), 0)
    row = iota((rows, 1), 0)
    for i in range(per_step):
        key = recv_ref[:, i, :, :hd].astype(F32)
        value = recv_ref[:, i, :, hd:].astype(F32)
        live = key[:, :, :1] < 0.5 * EMPTY
        key = jnp.sum(jnp.where(live, key, 0.0), axis=0)
        value = jnp.sum(value, axis=0)
        number = jnp.sum(jnp.where(live, 1.0, 0.0), axis=0)
        for e in range(CL_DEV):
            inside = (row >= e * cap) & (row < (e + 1) * cap)
            at = (step * per_step + i) * CL_DEV + e
            key_sum = jnp.sum(jnp.where(inside, key, 0.0), axis=0, keepdims=True)
            value_sum = jnp.sum(jnp.where(inside, value, 0.0), axis=0, keepdims=True)
            count = jnp.sum(jnp.where(inside, number, 0.0), axis=0, keepdims=True)
            here, there = line == at, line == at + owned
            acc_ref[...] += jnp.where(here, key_sum, jnp.where(there, value_sum, 0.0))
            count_ref[...] += jnp.where(here | there, count, 0.0)

    @pl.when(step == pl.num_programs(0) - 1)
    def _():
        count = count_ref[...]
        centers = acc_ref[...] / jnp.maximum(count, 1.0)
        r, l = iota((extra, hd), 0), iota((extra, hd), 1)
        diagonal = jnp.sum(jnp.where(r == l, count, 0.0), axis=0, keepdims=True)
        block = jnp.where(r == 2 * owned, diagonal, centers).astype(BF16)
        for j in range(n_seq):
            block_ref[j] = block
        copy = pltpu.make_async_copy(block_ref, send_ref.at[:, pl.ds(heads * rows, extra)], sem)
        copy.start()
        copy.wait()


def prepare_far(rank, all_centers, heads, key_ref, value_ref):
    _, far, _ = value_ref.shape
    n_seq, block, hd = all_centers.shape
    owned = heads * CL_DEV
    root = math.sqrt(hd)
    everything = all_centers.reshape(n_seq * block, hd)
    r, c = iota((far, n_seq * block), 1), iota((far, n_seq * block), 0)
    base = (c // CL_DEV) * block
    counts = nn_dot(one_zero(r == base + 2 * owned), everything)
    lane, line = iota((far, hd), 1), iota((far, hd), 0)
    cluster = line % CL_DEV
    own = (line // CL_DEV == rank) & (lane == cluster + 3)
    base = r - base - c % CL_DEV
    for h in range(heads):
        key = nn_dot(one_zero(base == h * CL_DEV), everything)
        value = nn_dot(one_zero(base == h * CL_DEV + owned), everything)
        count = jnp.sum(
            jnp.where(lane - cluster == h * CL_DEV, counts, 0.0), axis=1, keepdims=True
        )
        bias = jnp.where(count > 0, jnp.log(jnp.maximum(count, 1.0)) * root, NEG)
        high = bias.astype(BF16).astype(F32)
        middle = (bias - high).astype(BF16).astype(F32)
        low = bias - high - middle
        side = jnp.where(lane == 0, high, jnp.where(lane == 1, middle, jnp.where(lane == 2, low, 0.0)))
        side = jnp.where(own, NEG, side)
        key_ref[h, :, :hd] = key.astype(BF16)
        key_ref[h, :, hd:] = side.astype(BF16)
        value_ref[h, :, :hd] = value.astype(BF16)
        value_ref[h, :, hd:] = jnp.ones((far, hd), BF16)


def attend_kernel(rows, cap, rank_ref, recv_ref, near_key_ref, near_value_ref, out_ref, far_key_ref, far_value_ref):
    step = pl.program_id(0)
    n_seq, per_step = out_ref.shape[:2]
    hd = recv_ref.shape[2]
    heads = far_key_ref.shape[0]

    @pl.when(step == 0)
    def _():
        prepare_far(rank_ref[0], recv_ref[:, heads * rows :], heads, far_key_ref, far_value_ref)

    group = n_seq * 16
    scale = math.log2(math.e) / math.sqrt(hd)
    lane = iota((group, hd), 1)
    row = iota((n_seq, 16, 1), 1).reshape(group, 1)
    for i in range(per_step):
        h = step * per_step + i
        far_key, far_value = far_key_ref[h], far_value_ref[h]
        keys = [jnp.concatenate([near_key_ref[i, e], far_key], 0) for e in range(CL_DEV)]
        values = [jnp.concatenate([near_value_ref[i, e], far_value], 0) for e in range(CL_DEV)]
        for tile in range(rows // 16):
            place = row + tile * 16
            clusters = [
                e for e in range(CL_DEV) if e * cap < tile * 16 + 16 and (e + 1) * cap > tile * 16
            ]
            side = jnp.where(lane < 3, 1.0, 0.0)
            for e in clusters:
                inside = (place >= e * cap) & (place < (e + 1) * cap)
                side = jnp.where((lane == 3 + e) & inside, 1.0, side)
            start = pl.multiple_of(h * rows + tile * 16, 16)
            query = recv_ref[:, pl.ds(start, 16)].reshape(group, hd)
            query = jnp.concatenate([query, side.astype(BF16)], 1)
            score = None
            for e in clusters:
                mine = nt_dot(query, keys[e])
                score = mine if score is None else jnp.where(place >= e * cap, mine, score)
            top = jnp.max(score, 1, keepdims=True)
            weight = jnp.exp2((score - top) * scale).astype(BF16)
            mixed = None
            for e in clusters:
                mine = nn_dot(weight, values[e])
                mixed = mine if mixed is None else jnp.where(place >= e * cap, mine, mixed)
            answer = (mixed[:, :hd] / mixed[:, hd:]).astype(BF16)
            out_ref[:, i, tile * 16 : tile * 16 + 16] = answer.reshape(n_seq, 16, hd)


def unpack_kernel(column_ref, back_ref, out_ref):
    n_seq, per_step, rows, hd = back_ref.shape
    tok = out_ref.shape[0]
    slots = n_seq * rows
    h = pl.program_id(0) * per_step
    column = column_ref[...]
    for i in range(per_step):
        place = jnp.sum(
            jnp.where(iota((tok, 128), 1) == h + i, column, 0), axis=1, keepdims=True
        )
        hot = one_zero(iota((tok, slots), 1) == place)
        answer = nn_dot(hot, back_ref[:, i].reshape(slots, hd))
        out_ref[:, i * hd : (i + 1) * hd] = answer.astype(BF16)


def per_device(queries, keys, values, membership, w_out):
    n_seq = lax.axis_size("seq")
    groups = lax.axis_size("head")
    rank = lax.axis_index("seq")
    group = lax.axis_index("head")
    tok = queries.shape[0]
    heads = membership.shape[0]
    hd = queries.shape[1] // heads
    width = w_out.shape[1] // groups
    clusters = CL_DEV * n_seq
    cap = max(2, (2 * tok + clusters - 1) // clusters)
    rows = (CL_DEV * cap + 15) // 16 * 16
    near = n_seq * cap
    per_step = 2
    params = pltpu.CompilerParams(
        dimension_semantics=("arbitrary",),
        vmem_limit_bytes=60 * 1024 * 1024,
    )
    exchange = functools.partial(
        lax.all_to_all, axis_name="seq", split_axis=0, concat_axis=0, tiled=True
    )
    swap = [(i, (i + 1) % groups) for i in range(groups)]

    mine = lax.dynamic_slice_in_dim(w_out, group * width, width, 1)
    other = lax.dynamic_slice_in_dim(w_out, (1 - group) * width, width, 1)
    other = lax.ppermute(other, "head", swap)

    matrix = pl.BlockSpec((tok, per_step * hd), lambda h: (0, h))
    line = pl.BlockSpec((per_step, 1, tok), lambda h: (h, 0, 0))
    column = pl.BlockSpec((tok, 128), lambda h: (0, 0))

    def slot_block(depth, count):
        return pl.BlockSpec((n_seq, count, rows, depth), lambda h: (0, h, 0, 0))

    def slot_array(depth):
        return jax.ShapeDtypeStruct((n_seq, heads, rows, depth), BF16)

    send_kv, place = pl.pallas_call(
        functools.partial(pack_kv_kernel, rows, cap),
        grid=(heads // per_step,),
        in_specs=[line, matrix, matrix],
        out_specs=[slot_block(2 * hd, per_step), line],
        out_shape=[slot_array(2 * hd), jax.ShapeDtypeStruct((heads, 1, tok), jnp.int32)],
        scratch_shapes=[pltpu.VMEM((tok, tok), BF16)],
        compiler_params=params,
        name="pack_kv",
    )(membership.reshape(heads, 1, tok), keys, values)
    received_kv = exchange(send_kv)

    extra = (2 * heads * CL_DEV + 1 + 15) // 16 * 16
    all_rows = heads * rows + extra
    q_array = jax.ShapeDtypeStruct((n_seq, all_rows, hd), BF16)
    send_q, columns = pl.pallas_call(
        functools.partial(pack_q_kernel, rows),
        grid=(heads // per_step,),
        in_specs=[line, matrix],
        out_specs=[pl.BlockSpec((n_seq, per_step * rows, hd), lambda h: (0, h, 0)), column],
        out_shape=[q_array, jax.ShapeDtypeStruct((tok, 128), jnp.int32)],
        compiler_params=params,
        name="pack_q",
    )(place, queries)

    anywhere = pl.BlockSpec(memory_space=pl.ANY)
    send_q = pl.pallas_call(
        functools.partial(centers_kernel, cap, heads),
        grid=(heads // per_step,),
        in_specs=[slot_block(2 * hd, per_step), anywhere],
        out_specs=anywhere,
        out_shape=q_array,
        scratch_shapes=[
            pltpu.VMEM((extra, hd), F32),
            pltpu.VMEM((extra, 1), F32),
            pltpu.VMEM((n_seq, extra, hd), BF16),
            pltpu.SemaphoreType.DMA,
        ],
        input_output_aliases={1: 0},
        compiler_params=params,
        name="centers",
    )(received_kv, send_q)
    received_q = exchange(send_q)

    def near_block(count):
        return pl.BlockSpec((count, CL_DEV, near, 2 * hd), lambda h: (h, 0, 0, 0))

    near_array = jax.ShapeDtypeStruct((heads, CL_DEV, near, 2 * hd), BF16)
    near_keys, near_values = pl.pallas_call(
        functools.partial(regroup_kernel, rows, cap),
        grid=(heads,),
        in_specs=[slot_block(2 * hd, 1)],
        out_specs=[near_block(1), near_block(1)],
        out_shape=[near_array, near_array],
        scratch_shapes=[pltpu.VMEM((CL_DEV, near, n_seq * rows), BF16)],
        compiler_params=params,
        name="regroup",
    )(received_kv)

    answers = pl.pallas_call(
        functools.partial(attend_kernel, rows, cap),
        grid=(heads // per_step,),
        in_specs=[
            pl.BlockSpec(memory_space=pltpu.SMEM),
            pl.BlockSpec((n_seq, all_rows, hd), lambda h: (0, 0, 0)),
            near_block(per_step),
            near_block(per_step),
        ],
        out_specs=slot_block(hd, per_step),
        out_shape=slot_array(hd),
        scratch_shapes=[
            pltpu.VMEM((heads, clusters, 2 * hd), BF16),
            pltpu.VMEM((heads, clusters, 2 * hd), BF16),
        ],
        compiler_params=params,
        name="attend",
    )(rank.reshape(1), received_q, near_keys, near_values)
    returned = exchange(answers)

    attended = pl.pallas_call(
        unpack_kernel,
        grid=(heads // per_step,),
        in_specs=[column, slot_block(hd, per_step)],
        out_specs=matrix,
        out_shape=jax.ShapeDtypeStruct((tok, heads * hd), BF16),
        compiler_params=params,
        name="unpack",
    )(columns, returned)
    partner = lax.ppermute(attended, "head", swap)
    result = nn_dot(attended, mine) + nn_dot(partner, other)
    return result.astype(BF16)


def solution(mesh):
    return jax.shard_map(
        per_device,
        mesh=mesh,
        in_specs=(
            P("seq", "head"),
            P("seq", "head"),
            P("seq", "head"),
            P("head", "seq", None),
            P("head", None),
        ),
        out_specs=P("seq", "head"),
        check_vma=False,
    )
```

```python
import functools
import math

import jax
import jax.numpy as jnp
from jax import lax
from jax.experimental import pallas as pl
from jax.experimental.pallas import tpu as pltpu
from jax.sharding import PartitionSpec as P

CL_DEV = 4
NEG = -1e30
EMPTY = 128.0
BF16 = jnp.bfloat16
F32 = jnp.float32


def iota(shape, dim):
    return lax.broadcasted_iota(jnp.int32, shape, dim)


def nt_dot(a, b):
    return lax.dot_general(a, b, (((1,), (1,)), ((), ())), preferred_element_type=F32)


def nn_dot(a, b):
    return jnp.dot(a, b, preferred_element_type=F32)


def one_zero(mask, kind=BF16):
    return jnp.where(mask, 1.0, 0.0).astype(kind)


def pack_kv_kernel(rows, cap, member_ref, k_ref, v_ref, send_ref, place_ref, lower_ref):
    tok = k_ref.shape[0]
    n_seq, per_step = send_ref.shape[:2]
    hd = k_ref.shape[1] // per_step
    slots = n_seq * rows
    clusters = n_seq * CL_DEV

    @pl.when(pl.program_id(0) == 0)
    def _():
        lower_ref[...] = one_zero(iota((tok, tok), 0) < iota((tok, tok), 1))

    for i in range(per_step):
        member = member_ref[i]
        same = iota((clusters, tok), 0) == member
        before = nn_dot(one_zero(same), lower_ref[...])
        slot = jnp.sum(jnp.where(same, before, 0.0), axis=0, keepdims=True).astype(jnp.int32)
        place = (member // CL_DEV) * rows + (member % CL_DEV) * cap + slot
        place_ref[i] = place
        hot = one_zero(iota((slots, tok), 0) == place, F32)
        live = jnp.sum(hot, axis=1, keepdims=True)
        span = slice(i * hd, (i + 1) * hd)
        pair = jnp.concatenate([k_ref[:, span], v_ref[:, span]], 1)
        packed = nn_dot(hot.astype(BF16), pair)
        mark = jnp.where(iota((slots, hd), 1) == 0, EMPTY * (1.0 - live), 0.0)
        key = (packed[:, :hd] + mark).astype(BF16)
        send_ref[:, i, :, :hd] = key.reshape(n_seq, rows, hd)
        send_ref[:, i, :, hd:] = packed[:, hd:].astype(BF16).reshape(n_seq, rows, hd)


def pack_q_kernel(rows, place_ref, q_ref, send_ref, column_ref):
    tok = q_ref.shape[0]
    n_seq = send_ref.shape[0]
    per_step = send_ref.shape[1] // rows
    hd = q_ref.shape[1] // per_step
    slots = n_seq * rows
    h = pl.program_id(0) * per_step

    @pl.when(h == 0)
    def _():
        column_ref[...] = jnp.zeros_like(column_ref)

    for i in range(per_step):
        place = place_ref[i]
        hot = one_zero(iota((slots, tok), 0) == place)
        packed = nn_dot(hot, q_ref[:, i * hd : (i + 1) * hd])
        send_ref[:, i * rows : (i + 1) * rows] = packed.astype(BF16).reshape(n_seq, rows, hd)
        turned = jnp.broadcast_to(place.astype(F32), (128, tok)).T.astype(jnp.int32)
        column_ref[...] += jnp.where(iota((tok, 128), 1) == h + i, turned, 0)


def regroup_kernel(rows, cap, recv_ref, pair_ref, perm_ref):
    h = pl.program_id(0)
    n_seq = recv_ref.shape[0]
    slots = n_seq * rows
    near = n_seq * cap

    @pl.when(h == 0)
    def _():
        line = iota((near, 1), 0)
        source = line // cap
        origin = source * rows + (line - source * cap)
        for e in range(CL_DEV):
            perm_ref[e] = one_zero(iota((near, slots), 1) == origin + e * cap)

    pairs = recv_ref[:, 0].reshape(slots, recv_ref.shape[3])
    for e in range(CL_DEV):
        pair_ref[0, e] = nn_dot(perm_ref[e], pairs).astype(BF16)


def centers_kernel(cap, recv_ref, buffer_ref, send_ref, block_ref, sem):
    del buffer_ref
    n_seq, heads, rows, _ = recv_ref.shape
    _, extra, hd = block_ref.shape
    owned = heads * CL_DEV
    row = iota((rows, 1), 0)
    line = iota((extra, 1), 0)
    total = jnp.zeros((extra, hd), F32)
    count = jnp.zeros((extra, 1), F32)
    for h in range(heads):
        key = recv_ref[:, h, :, :hd].astype(F32)
        value = jnp.sum(recv_ref[:, h, :, hd:].astype(F32), axis=0)
        empty = key > 0.5 * EMPTY
        key = jnp.sum(jnp.where(empty, 0.0, key), axis=0)
        number = n_seq - jnp.sum(jnp.where(empty, 1.0, 0.0), axis=0)[:, :1]
        for e in range(CL_DEV):
            inside = (row >= e * cap) & (row < (e + 1) * cap)
            key_sum = jnp.sum(jnp.where(inside, key, 0.0), axis=0, keepdims=True)
            value_sum = jnp.sum(jnp.where(inside, value, 0.0), axis=0, keepdims=True)
            amount = jnp.sum(jnp.where(inside, number, 0.0), axis=0, keepdims=True)
            here, there = line == h * CL_DEV + e, line == h * CL_DEV + e + owned
            total = jnp.where(here, key_sum, jnp.where(there, value_sum, total))
            count = jnp.where(here | there, amount, count)
    centers = total / jnp.maximum(count, 1.0)
    r, l = iota((extra, hd), 0), iota((extra, hd), 1)
    diagonal = jnp.sum(jnp.where(r == l, count, 0.0), axis=0, keepdims=True)
    block = jnp.where(r == 2 * owned, diagonal, centers).astype(BF16)
    for j in range(n_seq):
        block_ref[j] = block
    copy = pltpu.make_async_copy(block_ref, send_ref.at[:, pl.ds(heads * rows, extra)], sem)
    copy.start()
    copy.wait()


def prepare_far(rank, all_centers, heads, key_ref, value_ref):
    _, far, _ = value_ref.shape
    n_seq, block, hd = all_centers.shape
    owned = heads * CL_DEV
    root = math.sqrt(hd)
    everything = all_centers.reshape(n_seq * block, hd)
    line = iota((far, 1), 0)
    base = (line // CL_DEV) * block
    cluster = line % CL_DEV

    def rows_at(offsets):
        wanted = jnp.concatenate([base + offset for offset in offsets], 0)
        return nn_dot(one_zero(iota((wanted.shape[0], n_seq * block), 1) == wanted), everything)

    counts = rows_at([2 * owned])
    offsets = [part * owned + h * CL_DEV + cluster for h in range(heads) for part in range(2)]
    if n_seq <= 16:
        means = rows_at(offsets)
        means = [means[i * far : (i + 1) * far] for i in range(len(offsets))]
    else:
        means = [rows_at([offset]) for offset in offsets]
    lane = iota((far, hd), 1)
    own = (line // CL_DEV == rank) & (lane == cluster + 3)
    for h in range(heads):
        count = jnp.sum(
            jnp.where(lane == cluster + h * CL_DEV, counts, 0.0), axis=1, keepdims=True
        )
        bias = jnp.where(count > 0, jnp.log(jnp.maximum(count, 1.0)) * root, NEG)
        high = bias.astype(BF16).astype(F32)
        middle = (bias - high).astype(BF16).astype(F32)
        low = bias - high - middle
        side = jnp.where(lane == 0, high, jnp.where(lane == 1, middle, jnp.where(lane == 2, low, 0.0)))
        side = jnp.where(own, NEG, side)
        key_ref[h, :, :hd] = means[2 * h].astype(BF16)
        key_ref[h, :, hd:] = side.astype(BF16)
        value_ref[h, :, :hd] = means[2 * h + 1].astype(BF16)
        value_ref[h, :, hd:] = jnp.ones((far, hd), BF16)


def tile_clusters(tile, rows, cap):
    ends = [(e + 1) * cap for e in range(CL_DEV - 1)] + [rows]
    return [e for e in range(CL_DEV) if e * cap < tile * 16 + 16 and ends[e] > tile * 16]


def attend_kernel(
    cap, rank_ref, q_ref, near_ref, out_ref,
    far_key_ref, far_value_ref, mask_ref, side_ref,
):
    step = pl.program_id(0)
    n_seq, per_step, rows, hd = out_ref.shape
    heads = far_key_ref.shape[0]
    group = n_seq * 16
    tiles = [tile_clusters(tile, rows, cap) for tile in range(rows // 16)]

    @pl.when(step == 0)
    def _():
        lane = iota((group, hd), 1)
        row = lax.rem(iota((group, hd), 0), 16)
        for tile, clusters in enumerate(tiles):
            place = row + tile * 16
            for j, e in enumerate(clusters):
                inside = place >= e * cap
                if e + 1 < CL_DEV:
                    inside = inside & (place < (e + 1) * cap)
                mask_ref[tile, j] = one_zero(inside)
                side_ref[tile, j] = one_zero(inside & ((lane < 3) | (lane == 3 + e)))
        prepare_far(rank_ref[0], q_ref[:, heads * rows :], heads, far_key_ref, far_value_ref)

    scale = math.log2(math.e) / math.sqrt(hd)
    for i in range(per_step):
        h = step * per_step + i
        far_key, far_value = far_key_ref[h], far_value_ref[h]
        keys, values = [], []
        for e in range(CL_DEV):
            key, value = near_ref[i, e, :, :hd], near_ref[i, e, :, hd:]
            side = jnp.where(key > 0.5 * EMPTY, NEG, 0.0).astype(BF16)
            keys.append(jnp.concatenate([jnp.concatenate([key, side], 1), far_key], 0))
            ones = jnp.ones(value.shape, BF16)
            values.append(jnp.concatenate([jnp.concatenate([value, ones], 1), far_value], 0))
        for tile, clusters in enumerate(tiles):
            start = pl.multiple_of(h * rows + tile * 16, 16)
            query = q_ref[:, pl.ds(start, 16)].reshape(group, hd)
            wide = []
            for j in range(len(clusters)):
                wide += [query * mask_ref[tile, j], side_ref[tile, j]]
            wide = jnp.concatenate(wide, 1)
            score = nt_dot(wide, jnp.concatenate([keys[e] for e in clusters], 1))
            top = jnp.max(score, 1, keepdims=True)
            weight = jnp.exp2((score - top) * scale).astype(BF16)
            repeat = weight.shape[1] // hd
            wide = [weight * jnp.concatenate([mask_ref[tile, j]] * repeat, 1) for j in range(len(clusters))]
            wide = jnp.concatenate(wide, 1)
            mixed = nn_dot(wide, jnp.concatenate([values[e] for e in clusters], 0))
            total = mixed[:, hd:]
            inverse = pl.reciprocal(total, approx=True)
            inverse = inverse * (2.0 - total * inverse)
            answer = (mixed[:, :hd] * inverse).astype(BF16)
            out_ref[:, i, tile * 16 : tile * 16 + 16] = answer.reshape(n_seq, 16, hd)


def unpack_kernel(column_ref, back_ref, out_ref):
    n_seq, per_step, rows, hd = back_ref.shape
    tok = out_ref.shape[0]
    slots = n_seq * rows
    h = pl.program_id(0) * per_step
    column = column_ref[...]
    for i in range(per_step):
        place = jnp.sum(
            jnp.where(iota((tok, 128), 1) == h + i, column, 0), axis=1, keepdims=True
        )
        hot = one_zero(iota((tok, slots), 1) == place)
        answer = nn_dot(hot, back_ref[:, i].reshape(slots, hd))
        out_ref[:, i * hd : (i + 1) * hd] = answer.astype(BF16)


def per_device(queries, keys, values, membership, w_out):
    n_seq = lax.axis_size("seq")
    groups = lax.axis_size("head")
    rank = lax.axis_index("seq")
    group = lax.axis_index("head")
    tok = queries.shape[0]
    heads = membership.shape[0]
    hd = queries.shape[1] // heads
    width = w_out.shape[1] // groups
    clusters = CL_DEV * n_seq
    cap = max(2, (2 * tok + clusters - 1) // clusters)
    rows = (CL_DEV * cap + 15) // 16 * 16
    near = n_seq * cap
    per_step = 2
    params = pltpu.CompilerParams(
        dimension_semantics=("arbitrary",),
        vmem_limit_bytes=60 * 1024 * 1024,
    )
    small = pltpu.CompilerParams(
        dimension_semantics=("arbitrary",),
        vmem_limit_bytes=(16 if n_seq <= 16 else 60) * 1024 * 1024,
    )
    exchange = functools.partial(
        lax.all_to_all, axis_name="seq", split_axis=0, concat_axis=0, tiled=True
    )
    swap = [(i, (i + 1) % groups) for i in range(groups)]

    mine = lax.dynamic_slice_in_dim(w_out, group * width, width, 1)
    other = lax.dynamic_slice_in_dim(w_out, (1 - group) * width, width, 1)
    other = lax.ppermute(other, "head", swap)

    matrix = pl.BlockSpec((tok, per_step * hd), lambda h: (0, h))
    line = pl.BlockSpec((per_step, 1, tok), lambda h: (h, 0, 0))
    column = pl.BlockSpec((tok, 128), lambda h: (0, 0))

    def slot_block(depth, count):
        return pl.BlockSpec((n_seq, count, rows, depth), lambda h: (0, h, 0, 0))

    def slot_array(depth):
        return jax.ShapeDtypeStruct((n_seq, heads, rows, depth), BF16)

    send_kv, place = pl.pallas_call(
        functools.partial(pack_kv_kernel, rows, cap),
        grid=(heads // per_step,),
        in_specs=[line, matrix, matrix],
        out_specs=[slot_block(2 * hd, per_step), line],
        out_shape=[slot_array(2 * hd), jax.ShapeDtypeStruct((heads, 1, tok), jnp.int32)],
        scratch_shapes=[pltpu.VMEM((tok, tok), BF16)],
        compiler_params=params,
        name="pack_kv",
    )(membership.reshape(heads, 1, tok), keys, values)
    received_kv = exchange(send_kv)

    extra = (2 * heads * CL_DEV + 1 + 31) // 32 * 32
    all_rows = heads * rows + extra
    q_array = jax.ShapeDtypeStruct((n_seq, all_rows, hd), BF16)
    q_block = pl.BlockSpec((n_seq, per_step * rows, hd), lambda h: (0, h, 0))
    send_q, columns = pl.pallas_call(
        functools.partial(pack_q_kernel, rows),
        grid=(heads // per_step,),
        in_specs=[line, matrix],
        out_specs=[q_block, column],
        out_shape=[q_array, jax.ShapeDtypeStruct((tok, 128), jnp.int32)],
        compiler_params=params,
        name="pack_q",
    )(place, queries)

    anywhere = pl.BlockSpec(memory_space=pl.ANY)
    in_vmem = pl.BlockSpec(memory_space=pltpu.VMEM)
    send_q = pl.pallas_call(
        functools.partial(centers_kernel, cap),
        in_specs=[in_vmem, anywhere],
        out_specs=anywhere,
        out_shape=q_array,
        scratch_shapes=[
            pltpu.VMEM((n_seq, extra, hd), BF16),
            pltpu.SemaphoreType.DMA,
        ],
        input_output_aliases={1: 0},
        compiler_params=pltpu.CompilerParams(vmem_limit_bytes=params.vmem_limit_bytes),
        name="centers",
    )(received_kv, send_q)
    received_q = exchange(send_q)

    def near_block(count):
        return pl.BlockSpec((count, CL_DEV, near, 2 * hd), lambda h: (h, 0, 0, 0))

    near_pairs = pl.pallas_call(
        functools.partial(regroup_kernel, rows, cap),
        grid=(heads,),
        in_specs=[slot_block(2 * hd, 1)],
        out_specs=near_block(1),
        out_shape=jax.ShapeDtypeStruct((heads, CL_DEV, near, 2 * hd), BF16),
        scratch_shapes=[pltpu.VMEM((CL_DEV, near, n_seq * rows), BF16)],
        compiler_params=params,
        name="regroup",
    )(received_kv)

    many = 3
    answers = pl.pallas_call(
        functools.partial(attend_kernel, cap),
        grid=(heads // many,),
        in_specs=[pl.BlockSpec(memory_space=pltpu.SMEM), in_vmem, near_block(many)],
        out_specs=slot_block(hd, many),
        out_shape=slot_array(hd),
        scratch_shapes=[
            pltpu.VMEM((heads, clusters, 2 * hd), BF16),
            pltpu.VMEM((heads, clusters, 2 * hd), BF16),
            pltpu.VMEM((rows // 16, CL_DEV, n_seq * 16, hd), BF16),
            pltpu.VMEM((rows // 16, CL_DEV, n_seq * 16, hd), BF16),
        ],
        compiler_params=params,
        name="attend",
    )(rank.reshape(1), received_q, near_pairs)
    returned = exchange(answers)

    attended = pl.pallas_call(
        unpack_kernel,
        grid=(heads // per_step,),
        in_specs=[column, slot_block(hd, per_step)],
        out_specs=matrix,
        out_shape=jax.ShapeDtypeStruct((tok, heads * hd), BF16),
        compiler_params=small,
        name="unpack",
    )(columns, returned)
    partner = lax.ppermute(attended, "head", swap)
    result = nn_dot(attended, mine) + nn_dot(partner, other)
    return result.astype(BF16)


def solution(mesh):
    return jax.shard_map(
        per_device,
        mesh=mesh,
        in_specs=(
            P("seq", "head"),
            P("seq", "head"),
            P("seq", "head"),
            P("head", "seq", None),
            P("head", None),
        ),
        out_specs=P("seq", "head"),
        check_vma=False,
    )
```

```python
import functools
import math

import jax
import jax.numpy as jnp
from jax import lax
from jax.experimental import pallas as pl
from jax.experimental.pallas import tpu as pltpu
from jax.sharding import PartitionSpec as P

CL_DEV = 4
NEG = -1e30
EMPTY = 128.0
BF16 = jnp.bfloat16
F32 = jnp.float32


def iota(shape, dim):
    return lax.broadcasted_iota(jnp.int32, shape, dim)


def nt_dot(a, b):
    return lax.dot_general(a, b, (((1,), (1,)), ((), ())), preferred_element_type=F32)


def nn_dot(a, b):
    return jnp.dot(a, b, preferred_element_type=F32)


def one_zero(mask, kind=BF16):
    return jnp.where(mask, 1.0, 0.0).astype(kind)


def pack_kv_kernel(rows, cap, member_ref, k_ref, v_ref, send_ref, place_ref, lower_ref):
    tok = k_ref.shape[0]
    n_seq, per_step = send_ref.shape[:2]
    hd = k_ref.shape[1] // per_step
    slots = n_seq * rows
    clusters = n_seq * CL_DEV

    @pl.when(pl.program_id(0) == 0)
    def _():
        lower_ref[...] = one_zero(iota((tok, tok), 0) < iota((tok, tok), 1))

    for i in range(per_step):
        member = member_ref[i]
        same = iota((clusters, tok), 0) == member
        before = nn_dot(one_zero(same), lower_ref[...])
        slot = jnp.sum(jnp.where(same, before, 0.0), axis=0, keepdims=True).astype(jnp.int32)
        place = (member // CL_DEV) * rows + (member % CL_DEV) * cap + slot
        place_ref[i] = place
        hot = one_zero(iota((slots, tok), 0) == place, F32)
        live = jnp.sum(hot, axis=1, keepdims=True)
        span = slice(i * hd, (i + 1) * hd)
        pair = jnp.concatenate([k_ref[:, span], v_ref[:, span]], 1)
        packed = nn_dot(hot.astype(BF16), pair)
        mark = jnp.where(iota((slots, hd), 1) == 0, EMPTY * (1.0 - live), 0.0)
        key = (packed[:, :hd] + mark).astype(BF16)
        send_ref[:, i, :, :hd] = key.reshape(n_seq, rows, hd)
        send_ref[:, i, :, hd:] = packed[:, hd:].astype(BF16).reshape(n_seq, rows, hd)


def pack_q_kernel(rows, place_ref, q_ref, send_ref, column_ref):
    tok = q_ref.shape[0]
    n_seq = send_ref.shape[0]
    per_step = send_ref.shape[1] // rows
    hd = q_ref.shape[1] // per_step
    slots = n_seq * rows
    h = pl.program_id(0) * per_step

    @pl.when(h == 0)
    def _():
        column_ref[...] = jnp.zeros_like(column_ref)

    for i in range(per_step):
        place = place_ref[i]
        hot = one_zero(iota((slots, tok), 0) == place)
        packed = nn_dot(hot, q_ref[:, i * hd : (i + 1) * hd])
        send_ref[:, i * rows : (i + 1) * rows] = packed.astype(BF16).reshape(n_seq, rows, hd)
        turned = jnp.broadcast_to(place.astype(F32), (128, tok)).T.astype(jnp.int32)
        column_ref[...] += jnp.where(iota((tok, 128), 1) == h + i, turned, 0)


def regroup_kernel(rows, cap, recv_ref, pair_ref, perm_ref):
    h = pl.program_id(0)
    n_seq = recv_ref.shape[0]
    slots = n_seq * rows
    near = n_seq * cap

    @pl.when(h == 0)
    def _():
        line = iota((near, 1), 0)
        source = line // cap
        origin = source * rows + (line - source * cap)
        for e in range(CL_DEV):
            perm_ref[e] = one_zero(iota((near, slots), 1) == origin + e * cap)

    pairs = recv_ref[:, 0].reshape(slots, recv_ref.shape[3])
    for e in range(CL_DEV):
        pair_ref[0, e] = nn_dot(perm_ref[e], pairs).astype(BF16)


def centers_kernel(cap, recv_hbm, buffer_ref, send_ref, recv_ref, block_ref, in_sem, sem):
    del buffer_ref
    n_seq, heads, rows, _ = recv_ref.shape
    incoming = [
        pltpu.make_async_copy(recv_hbm.at[:, h], recv_ref.at[:, h], in_sem.at[h]) for h in range(heads)
    ]
    for copy in incoming:
        copy.start()
    _, extra, hd = block_ref.shape
    owned = heads * CL_DEV
    row = iota((rows, 1), 0)
    line = iota((extra, 1), 0)
    total = jnp.zeros((extra, hd), F32)
    count = jnp.zeros((extra, 1), F32)
    for h in range(heads):
        incoming[h].wait()
        key = recv_ref[:, h, :, :hd].astype(F32)
        value = jnp.sum(recv_ref[:, h, :, hd:].astype(F32), axis=0)
        empty = key > 0.5 * EMPTY
        key = jnp.sum(jnp.where(empty, 0.0, key), axis=0)
        number = n_seq - jnp.sum(jnp.where(empty, 1.0, 0.0), axis=0)[:, :1]
        for e in range(CL_DEV):
            inside = (row >= e * cap) & (row < (e + 1) * cap)
            key_sum = jnp.sum(jnp.where(inside, key, 0.0), axis=0, keepdims=True)
            value_sum = jnp.sum(jnp.where(inside, value, 0.0), axis=0, keepdims=True)
            amount = jnp.sum(jnp.where(inside, number, 0.0), axis=0, keepdims=True)
            here, there = line == h * CL_DEV + e, line == h * CL_DEV + e + owned
            total = jnp.where(here, key_sum, jnp.where(there, value_sum, total))
            count = jnp.where(here | there, amount, count)
    centers = total / jnp.maximum(count, 1.0)
    r, l = iota((extra, hd), 0), iota((extra, hd), 1)
    diagonal = jnp.sum(jnp.where(r == l, count, 0.0), axis=0, keepdims=True)
    block = jnp.where(r == 2 * owned, diagonal, centers).astype(BF16)
    for j in range(n_seq):
        block_ref[j] = block
    copy = pltpu.make_async_copy(block_ref, send_ref.at[:, pl.ds(heads * rows, extra)], sem)
    copy.start()
    copy.wait()


def prepare_far(rank, all_centers, heads, key_ref, value_ref):
    _, far, _ = value_ref.shape
    n_seq, block, hd = all_centers.shape
    owned = heads * CL_DEV
    root = math.sqrt(hd)
    everything = all_centers.reshape(n_seq * block, hd)
    line = iota((far, 1), 0)
    base = (line // CL_DEV) * block
    cluster = line % CL_DEV

    def rows_at(offsets):
        wanted = jnp.concatenate([base + offset for offset in offsets], 0)
        return nn_dot(one_zero(iota((wanted.shape[0], n_seq * block), 1) == wanted), everything)

    counts = rows_at([2 * owned])
    offsets = [part * owned + h * CL_DEV + cluster for h in range(heads) for part in range(2)]
    if n_seq <= 16:
        means = rows_at(offsets)
        means = [means[i * far : (i + 1) * far] for i in range(len(offsets))]
    else:
        means = [rows_at([offset]) for offset in offsets]
    lane = iota((far, hd), 1)
    own = (line // CL_DEV == rank) & (lane == cluster + 3)
    for h in range(heads):
        count = jnp.sum(
            jnp.where(lane == cluster + h * CL_DEV, counts, 0.0), axis=1, keepdims=True
        )
        bias = jnp.where(count > 0, jnp.log(jnp.maximum(count, 1.0)) * root, NEG)
        high = bias.astype(BF16).astype(F32)
        middle = (bias - high).astype(BF16).astype(F32)
        low = bias - high - middle
        side = jnp.where(lane == 0, high, jnp.where(lane == 1, middle, jnp.where(lane == 2, low, 0.0)))
        side = jnp.where(own, NEG, side)
        key_ref[h, :, :hd] = means[2 * h].astype(BF16)
        key_ref[h, :, hd:] = side.astype(BF16)
        value_ref[h, :, :hd] = means[2 * h + 1].astype(BF16)
        value_ref[h, :, hd:] = jnp.ones((far, hd), BF16)


def tile_clusters(tile, rows, cap):
    ends = [(e + 1) * cap for e in range(CL_DEV - 1)] + [rows]
    return [e for e in range(CL_DEV) if e * cap < tile * 16 + 16 and ends[e] > tile * 16]


def attend_kernel(
    cap, rank_ref, q_ref, near_ref, out_ref,
    far_key_ref, far_value_ref, mask_ref, side_ref,
):
    step = pl.program_id(0)
    n_seq, per_step, rows, hd = out_ref.shape
    heads = far_key_ref.shape[0]
    group = n_seq * 16
    tiles = [tile_clusters(tile, rows, cap) for tile in range(rows // 16)]

    @pl.when(step == 0)
    def _():
        lane = iota((group, hd), 1)
        row = lax.rem(iota((group, hd), 0), 16)
        for tile, clusters in enumerate(tiles):
            place = row + tile * 16
            for j, e in enumerate(clusters):
                inside = place >= e * cap
                if e + 1 < CL_DEV:
                    inside = inside & (place < (e + 1) * cap)
                mask_ref[tile, j] = one_zero(inside)
                side_ref[tile, j] = one_zero(inside & ((lane < 3) | (lane == 3 + e)))
        prepare_far(rank_ref[0], q_ref[:, heads * rows :], heads, far_key_ref, far_value_ref)

    scale = math.log2(math.e) / math.sqrt(hd)
    for i in range(per_step):
        h = step * per_step + i
        far_key, far_value = far_key_ref[h], far_value_ref[h]
        keys, values = [], []
        for e in range(CL_DEV):
            key, value = near_ref[i, e, :, :hd], near_ref[i, e, :, hd:]
            side = jnp.where(key > 0.5 * EMPTY, NEG, 0.0).astype(BF16)
            keys.append(jnp.concatenate([jnp.concatenate([key, side], 1), far_key], 0))
            ones = jnp.ones(value.shape, BF16)
            values.append(jnp.concatenate([jnp.concatenate([value, ones], 1), far_value], 0))
        for tile, clusters in enumerate(tiles):
            start = pl.multiple_of(h * rows + tile * 16, 16)
            query = q_ref[:, pl.ds(start, 16)].reshape(group, hd)
            wide = []
            for j in range(len(clusters)):
                wide += [query * mask_ref[tile, j], side_ref[tile, j]]
            wide = jnp.concatenate(wide, 1)
            score = nt_dot(wide, jnp.concatenate([keys[e] for e in clusters], 1))
            top = jnp.max(score, 1, keepdims=True)
            weight = jnp.exp2((score - top) * scale).astype(BF16)
            repeat = weight.shape[1] // hd
            wide = [weight * jnp.concatenate([mask_ref[tile, j]] * repeat, 1) for j in range(len(clusters))]
            wide = jnp.concatenate(wide, 1)
            mixed = nn_dot(wide, jnp.concatenate([values[e] for e in clusters], 0))
            total = mixed[:, hd:]
            inverse = pl.reciprocal(total, approx=True)
            inverse = inverse * (2.0 - total * inverse)
            answer = (mixed[:, :hd] * inverse).astype(BF16)
            out_ref[:, i, tile * 16 : tile * 16 + 16] = answer.reshape(n_seq, 16, hd)


def unpack_kernel(column_ref, back_ref, out_ref):
    n_seq, per_step, rows, hd = back_ref.shape
    tok = out_ref.shape[0]
    slots = n_seq * rows
    h = pl.program_id(0) * per_step
    column = column_ref[...]
    for i in range(per_step):
        place = jnp.sum(
            jnp.where(iota((tok, 128), 1) == h + i, column, 0), axis=1, keepdims=True
        )
        lane = lax.broadcasted_iota(jnp.int16, (tok, slots), 1)
        hot = jnp.where(lane == place.astype(jnp.int16), jnp.ones(lane.shape, BF16), jnp.zeros(lane.shape, BF16))
        answer = nn_dot(hot, back_ref[:, i].reshape(slots, hd))
        out_ref[:, i * hd : (i + 1) * hd] = answer.astype(BF16)


def own_part_kernel(attended_ref, mine_ref, other_ref, part_ref, staged_ref):
    part_ref[...] = nn_dot(attended_ref[...], mine_ref[...])
    staged_ref[...] = other_ref[...]


def finish_kernel(part_ref, partner_ref, weight_ref, out_ref):
    out_ref[...] = (part_ref[...] + nn_dot(partner_ref[...], weight_ref[...])).astype(BF16)


def per_device(queries, keys, values, membership, w_out):
    n_seq = lax.axis_size("seq")
    groups = lax.axis_size("head")
    rank = lax.axis_index("seq")
    group = lax.axis_index("head")
    tok = queries.shape[0]
    heads = membership.shape[0]
    hd = queries.shape[1] // heads
    width = w_out.shape[1] // groups
    clusters = CL_DEV * n_seq
    cap = max(2, (2 * tok + clusters - 1) // clusters)
    rows = (CL_DEV * cap + 15) // 16 * 16
    near = n_seq * cap
    per_step = 2
    params = pltpu.CompilerParams(
        dimension_semantics=("arbitrary",),
        vmem_limit_bytes=63 * 1024 * 1024,
    )
    small = pltpu.CompilerParams(
        dimension_semantics=("arbitrary",),
        vmem_limit_bytes=(16 if n_seq <= 16 else 60) * 1024 * 1024,
    )
    exchange = functools.partial(
        lax.all_to_all, axis_name="seq", split_axis=0, concat_axis=0, tiled=True
    )
    swap = [(i, (i + 1) % groups) for i in range(groups)]

    mine = lax.dynamic_slice_in_dim(w_out, group * width, width, 1)
    other = lax.dynamic_slice_in_dim(w_out, (1 - group) * width, width, 1)
    other = lax.ppermute(other, "head", swap)

    matrix = pl.BlockSpec((tok, per_step * hd), lambda h: (0, h))
    line = pl.BlockSpec((per_step, 1, tok), lambda h: (h, 0, 0))
    column = pl.BlockSpec((tok, 128), lambda h: (0, 0))

    def slot_block(depth, count):
        return pl.BlockSpec((n_seq, count, rows, depth), lambda h: (0, h, 0, 0))

    def slot_array(depth):
        return jax.ShapeDtypeStruct((n_seq, heads, rows, depth), BF16)

    anywhere = pl.BlockSpec(memory_space=pl.ANY)
    in_vmem = pl.BlockSpec(memory_space=pltpu.VMEM)
    whole_params = pltpu.CompilerParams(vmem_limit_bytes=params.vmem_limit_bytes)
    send_kv, place = pl.pallas_call(
        functools.partial(pack_kv_kernel, rows, cap),
        grid=(heads // per_step,),
        in_specs=[line, matrix, matrix],
        out_specs=[slot_block(2 * hd, per_step), line],
        out_shape=[slot_array(2 * hd), jax.ShapeDtypeStruct((heads, 1, tok), jnp.int32)],
        scratch_shapes=[pltpu.VMEM((tok, tok), BF16)],
        compiler_params=params,
        name="pack_kv",
    )(membership.reshape(heads, 1, tok), keys, values)
    received_kv = exchange(send_kv)

    extra = (2 * heads * CL_DEV + 1 + 31) // 32 * 32
    all_rows = heads * rows + extra
    q_array = jax.ShapeDtypeStruct((n_seq, all_rows, hd), BF16)
    q_block = pl.BlockSpec((n_seq, per_step * rows, hd), lambda h: (0, h, 0))
    send_q, columns = pl.pallas_call(
        functools.partial(pack_q_kernel, rows),
        grid=(heads // per_step,),
        in_specs=[line, matrix],
        out_specs=[q_block, column],
        out_shape=[q_array, jax.ShapeDtypeStruct((tok, 128), jnp.int32)],
        compiler_params=params,
        name="pack_q",
    )(place, queries)

    send_q = pl.pallas_call(
        functools.partial(centers_kernel, cap),
        in_specs=[anywhere, anywhere],
        out_specs=anywhere,
        out_shape=q_array,
        scratch_shapes=[
            pltpu.VMEM((n_seq, heads, rows, 2 * hd), BF16),
            pltpu.VMEM((n_seq, extra, hd), BF16),
            pltpu.SemaphoreType.DMA((heads,)),
            pltpu.SemaphoreType.DMA,
        ],
        input_output_aliases={1: 0},
        compiler_params=whole_params,
        name="centers",
    )(received_kv, send_q)
    received_q = exchange(send_q)

    def near_block(count):
        return pl.BlockSpec((count, CL_DEV, near, 2 * hd), lambda h: (h, 0, 0, 0))

    near_pairs = pl.pallas_call(
        functools.partial(regroup_kernel, rows, cap),
        grid=(heads,),
        in_specs=[slot_block(2 * hd, 1)],
        out_specs=near_block(1),
        out_shape=jax.ShapeDtypeStruct((heads, CL_DEV, near, 2 * hd), BF16),
        scratch_shapes=[pltpu.VMEM((CL_DEV, near, n_seq * rows), BF16)],
        compiler_params=params,
        name="regroup",
    )(received_kv)

    many = 3
    answers = pl.pallas_call(
        functools.partial(attend_kernel, cap),
        grid=(heads // many,),
        in_specs=[pl.BlockSpec(memory_space=pltpu.SMEM), in_vmem, near_block(many)],
        out_specs=slot_block(hd, many),
        out_shape=slot_array(hd),
        scratch_shapes=[
            pltpu.VMEM((heads, clusters, 2 * hd), BF16),
            pltpu.VMEM((heads, clusters, 2 * hd), BF16),
            pltpu.VMEM((rows // 16, CL_DEV, n_seq * 16, hd), BF16),
            pltpu.VMEM((rows // 16, CL_DEV, n_seq * 16, hd), BF16),
        ],
        compiler_params=params,
        name="attend",
    )(rank.reshape(1), received_q, near_pairs)
    returned = exchange(answers)

    attended = pl.pallas_call(
        unpack_kernel,
        grid=(heads // many,),
        in_specs=[column, slot_block(hd, many)],
        out_specs=pl.BlockSpec((tok, many * hd), lambda h: (0, h)),
        out_shape=jax.ShapeDtypeStruct((tok, heads * hd), BF16),
        compiler_params=small,
        name="unpack",
    )(columns, returned)
    partner = lax.ppermute(attended, "head", swap)
    tail = pltpu.CompilerParams(vmem_limit_bytes=16 * 1024 * 1024)
    own_part, staged = pl.pallas_call(
        own_part_kernel,
        in_specs=[in_vmem] * 3,
        out_specs=[in_vmem] * 2,
        out_shape=[
            jax.ShapeDtypeStruct((tok, width), F32),
            jax.ShapeDtypeStruct(other.shape, BF16),
        ],
        compiler_params=tail,
        name="own_part",
    )(attended, mine, other)
    return pl.pallas_call(
        finish_kernel,
        in_specs=[in_vmem] * 3,
        out_specs=in_vmem,
        out_shape=jax.ShapeDtypeStruct((tok, width), BF16),
        compiler_params=tail,
        name="finish",
    )(own_part, partner, staged)


def solution(mesh):
    return jax.shard_map(
        per_device,
        mesh=mesh,
        in_specs=(
            P("seq", "head"),
            P("seq", "head"),
            P("seq", "head"),
            P("head", "seq", None),
            P("head", None),
        ),
        out_specs=P("seq", "head"),
        check_vma=False,
    )
```

```python
import functools
import math

import jax
import jax.numpy as jnp
from jax import lax
from jax.experimental import pallas as pl
from jax.experimental.pallas import tpu as pltpu
from jax.sharding import PartitionSpec as P

CL_DEV = 4
NEG = -1e30
EMPTY = 128.0
BF16 = jnp.bfloat16
F32 = jnp.float32


def iota(shape, dim):
    return lax.broadcasted_iota(jnp.int32, shape, dim)


def nt_dot(a, b):
    return lax.dot_general(a, b, (((1,), (1,)), ((), ())), preferred_element_type=F32)


def nn_dot(a, b):
    return jnp.dot(a, b, preferred_element_type=F32)


def one_zero(mask, kind=BF16):
    return jnp.where(mask, 1.0, 0.0).astype(kind)


def pack_kv_kernel(rows, cap, member_ref, k_ref, v_ref, send_ref, place_ref, lower_ref):
    tok = k_ref.shape[0]
    n_seq, per_step = send_ref.shape[:2]
    hd = k_ref.shape[1] // per_step
    slots = n_seq * rows
    clusters = n_seq * CL_DEV

    @pl.when(pl.program_id(0) == 0)
    def _():
        lower_ref[...] = one_zero(iota((tok, tok), 0) < iota((tok, tok), 1))

    for i in range(per_step):
        member = member_ref[i]
        same = iota((clusters, tok), 0) == member
        before = nn_dot(one_zero(same), lower_ref[...])
        slot = jnp.sum(jnp.where(same, before, 0.0), axis=0, keepdims=True).astype(jnp.int32)
        place = (member // CL_DEV) * rows + (member % CL_DEV) * cap + slot
        place_ref[i] = place
        hot = one_zero(iota((slots, tok), 0) == place, F32)
        live = jnp.sum(hot, axis=1, keepdims=True)
        span = slice(i * hd, (i + 1) * hd)
        pair = jnp.concatenate([k_ref[:, span], v_ref[:, span]], 1)
        packed = nn_dot(hot.astype(BF16), pair)
        mark = jnp.where(iota((slots, hd), 1) == 0, EMPTY * (1.0 - live), 0.0)
        key = (packed[:, :hd] + mark).astype(BF16)
        send_ref[:, i, :, :hd] = key.reshape(n_seq, rows, hd)
        send_ref[:, i, :, hd:] = packed[:, hd:].astype(BF16).reshape(n_seq, rows, hd)


def pack_q_kernel(rows, place_ref, q_ref, send_ref, column_ref):
    tok = q_ref.shape[0]
    n_seq = send_ref.shape[0]
    per_step = send_ref.shape[1] // rows
    hd = q_ref.shape[1] // per_step
    slots = n_seq * rows
    h = pl.program_id(0) * per_step

    @pl.when(h == 0)
    def _():
        column_ref[...] = jnp.zeros_like(column_ref)

    for i in range(per_step):
        place = place_ref[i]
        hot = one_zero(iota((slots, tok), 0) == place)
        packed = nn_dot(hot, q_ref[:, i * hd : (i + 1) * hd])
        send_ref[:, i * rows : (i + 1) * rows] = packed.astype(BF16).reshape(n_seq, rows, hd)
        turned = jnp.broadcast_to(place.astype(F32), (128, tok)).T.astype(jnp.int32)
        column_ref[...] += jnp.where(iota((tok, 128), 1) == h + i, turned, 0)


def regroup_kernel(rows, cap, recv_ref, pair_ref, perm_ref):
    h = pl.program_id(0)
    n_seq = recv_ref.shape[0]
    slots = n_seq * rows
    near = n_seq * cap

    @pl.when(h == 0)
    def _():
        line = iota((near, 1), 0)
        source = line // cap
        origin = source * rows + (line - source * cap)
        for e in range(CL_DEV):
            perm_ref[e] = one_zero(iota((near, slots), 1) == origin + e * cap)

    pairs = recv_ref[:, 0].reshape(slots, recv_ref.shape[3])
    for e in range(CL_DEV):
        pair_ref[0, e] = nn_dot(perm_ref[e], pairs).astype(BF16)


def centers_kernel(cap, recv_hbm, buffer_ref, send_ref, recv_ref, block_ref, in_sem, sem):
    del buffer_ref
    n_seq, heads, rows, _ = recv_ref.shape
    incoming = [
        pltpu.make_async_copy(recv_hbm.at[:, h], recv_ref.at[:, h], in_sem.at[h]) for h in range(heads)
    ]
    for copy in incoming:
        copy.start()
    _, extra, hd = block_ref.shape
    owned = heads * CL_DEV
    row = iota((rows, 1), 0)
    line = iota((extra, 1), 0)
    total = jnp.zeros((extra, hd), F32)
    count = jnp.zeros((extra, 1), F32)
    for h in range(heads):
        incoming[h].wait()
        key = recv_ref[:, h, :, :hd].astype(F32)
        value = jnp.sum(recv_ref[:, h, :, hd:].astype(F32), axis=0)
        empty = key > 0.5 * EMPTY
        key = jnp.sum(jnp.where(empty, 0.0, key), axis=0)
        number = n_seq - jnp.sum(jnp.where(empty, 1.0, 0.0), axis=0)[:, :1]
        for e in range(CL_DEV):
            inside = (row >= e * cap) & (row < (e + 1) * cap)
            key_sum = jnp.sum(jnp.where(inside, key, 0.0), axis=0, keepdims=True)
            value_sum = jnp.sum(jnp.where(inside, value, 0.0), axis=0, keepdims=True)
            amount = jnp.sum(jnp.where(inside, number, 0.0), axis=0, keepdims=True)
            here, there = line == h * CL_DEV + e, line == h * CL_DEV + e + owned
            total = jnp.where(here, key_sum, jnp.where(there, value_sum, total))
            count = jnp.where(here | there, amount, count)
    centers = total / jnp.maximum(count, 1.0)
    r, l = iota((extra, hd), 0), iota((extra, hd), 1)
    diagonal = jnp.sum(jnp.where(r == l, count, 0.0), axis=0, keepdims=True)
    block = jnp.where(r == 2 * owned, diagonal, centers).astype(BF16)
    for j in range(n_seq):
        block_ref[j] = block
    copy = pltpu.make_async_copy(block_ref, send_ref.at[:, pl.ds(heads * rows, extra)], sem)
    copy.start()
    copy.wait()


def prepare_far(rank, all_centers, heads, key_ref, value_ref):
    _, far, _ = value_ref.shape
    n_seq, block, hd = all_centers.shape
    owned = heads * CL_DEV
    root = math.sqrt(hd)
    everything = all_centers.reshape(n_seq * block, hd)
    line = iota((far, 1), 0)
    base = (line // CL_DEV) * block
    cluster = line % CL_DEV

    def rows_at(offsets):
        wanted = jnp.concatenate([base + offset for offset in offsets], 0)
        return nn_dot(one_zero(iota((wanted.shape[0], n_seq * block), 1) == wanted), everything)

    counts = rows_at([2 * owned])
    offsets = [part * owned + h * CL_DEV + cluster for h in range(heads) for part in range(2)]
    if n_seq <= 16:
        means = rows_at(offsets)
        means = [means[i * far : (i + 1) * far] for i in range(len(offsets))]
    else:
        means = [rows_at([offset]) for offset in offsets]
    lane = iota((far, hd), 1)
    own = (line // CL_DEV == rank) & (lane == cluster + 3)
    for h in range(heads):
        count = jnp.sum(
            jnp.where(lane == cluster + h * CL_DEV, counts, 0.0), axis=1, keepdims=True
        )
        bias = jnp.where(count > 0, jnp.log(jnp.maximum(count, 1.0)) * root, NEG)
        high = bias.astype(BF16).astype(F32)
        middle = (bias - high).astype(BF16).astype(F32)
        low = bias - high - middle
        side = jnp.where(lane == 0, high, jnp.where(lane == 1, middle, jnp.where(lane == 2, low, 0.0)))
        side = jnp.where(own, NEG, side)
        key_ref[h, :, :hd] = means[2 * h].astype(BF16)
        key_ref[h, :, hd:] = side.astype(BF16)
        value_ref[h, :, :hd] = means[2 * h + 1].astype(BF16)
        value_ref[h, :, hd:] = jnp.ones((far, hd), BF16)


def tile_clusters(tile, rows, cap):
    ends = [(e + 1) * cap for e in range(CL_DEV - 1)] + [rows]
    return [e for e in range(CL_DEV) if e * cap < tile * 16 + 16 and ends[e] > tile * 16]


def attend_kernel(
    cap, rank_ref, q_hbm, near_hbm, out_hbm, far_key_ref, far_value_ref, mask_ref, side_ref,
    q_ref, near_ref, out_ref, q_sem, in_sem, out_sem,
):
    n_seq, heads, rows, hd = out_ref.shape
    group = n_seq * 16
    tiles = [tile_clusters(tile, rows, cap) for tile in range(rows // 16)]
    incoming, outgoing = [], []
    for h in range(heads):
        incoming.append(pltpu.make_async_copy(near_hbm.at[h], near_ref.at[h], in_sem.at[h]))
        outgoing.append(pltpu.make_async_copy(out_ref.at[:, h], out_hbm.at[:, h], out_sem.at[h]))
    split = heads * rows
    means, slots = pl.ds(split, q_ref.shape[1] - split), pl.ds(0, split)
    means = pltpu.make_async_copy(q_hbm.at[:, means], q_ref.at[:, means], q_sem.at[0])
    slots = pltpu.make_async_copy(q_hbm.at[:, slots], q_ref.at[:, slots], q_sem.at[1])
    means.start()
    slots.start()
    for copy in incoming:
        copy.start()

    lane = iota((group, hd), 1)
    row = lax.rem(iota((group, hd), 0), 16)
    for tile, clusters in enumerate(tiles):
        place = row + tile * 16
        for j, e in enumerate(clusters):
            inside = place >= e * cap
            if e + 1 < CL_DEV:
                inside = inside & (place < (e + 1) * cap)
            mask_ref[tile, j] = one_zero(inside)
            side_ref[tile, j] = one_zero(inside & ((lane < 3) | (lane == 3 + e)))
    means.wait()
    prepare_far(rank_ref[0], q_ref[:, heads * rows :], heads, far_key_ref, far_value_ref)
    slots.wait()
    for copy in incoming:
        copy.wait()

    scale = math.log2(math.e) / math.sqrt(hd)
    for h in range(heads):
        far_key, far_value = far_key_ref[h], far_value_ref[h]
        keys, values = [], []
        for e in range(CL_DEV):
            key, value = near_ref[h, e, :, :hd], near_ref[h, e, :, hd:]
            side = jnp.where(key > 0.5 * EMPTY, NEG, 0.0).astype(BF16)
            keys.append(jnp.concatenate([jnp.concatenate([key, side], 1), far_key], 0))
            ones = jnp.ones(value.shape, BF16)
            values.append(jnp.concatenate([jnp.concatenate([value, ones], 1), far_value], 0))
        for tile, clusters in enumerate(tiles):
            start = h * rows + tile * 16
            query = q_ref[:, start : start + 16].reshape(group, hd)
            wide = []
            for j in range(len(clusters)):
                wide += [query * mask_ref[tile, j], side_ref[tile, j]]
            wide = jnp.concatenate(wide, 1)
            score = nt_dot(wide, jnp.concatenate([keys[e] for e in clusters], 1))
            top = jnp.max(score, 1, keepdims=True)
            weight = jnp.exp2((score - top) * scale).astype(BF16)
            repeat = weight.shape[1] // hd
            wide = [weight * jnp.concatenate([mask_ref[tile, j]] * repeat, 1) for j in range(len(clusters))]
            wide = jnp.concatenate(wide, 1)
            mixed = nn_dot(wide, jnp.concatenate([values[e] for e in clusters], 0))
            total = mixed[:, hd:]
            inverse = pl.reciprocal(total, approx=True)
            inverse = inverse * (2.0 - total * inverse)
            answer = (mixed[:, :hd] * inverse).astype(BF16)
            out_ref[:, h, tile * 16 : tile * 16 + 16] = answer.reshape(n_seq, 16, hd)
        outgoing[h].start()
    for copy in outgoing:
        copy.wait()


def unpack_kernel(column_ref, back_ref, out_ref):
    n_seq, per_step, rows, hd = back_ref.shape
    tok = out_ref.shape[0]
    slots = n_seq * rows
    h = pl.program_id(0) * per_step
    column = column_ref[...]
    for i in range(per_step):
        place = jnp.sum(
            jnp.where(iota((tok, 128), 1) == h + i, column, 0), axis=1, keepdims=True
        )
        lane = lax.broadcasted_iota(jnp.int16, (tok, slots), 1)
        hot = jnp.where(lane == place.astype(jnp.int16), jnp.ones(lane.shape, BF16), jnp.zeros(lane.shape, BF16))
        answer = nn_dot(hot, back_ref[:, i].reshape(slots, hd))
        out_ref[:, i * hd : (i + 1) * hd] = answer.astype(BF16)


def own_part_kernel(attended_ref, mine_ref, other_ref, part_ref, staged_ref):
    part_ref[...] = nn_dot(attended_ref[...], mine_ref[...])
    staged_ref[...] = other_ref[...]


def finish_kernel(part_ref, partner_ref, weight_ref, out_ref):
    out_ref[...] = (part_ref[...] + nn_dot(partner_ref[...], weight_ref[...])).astype(BF16)


def per_device(queries, keys, values, membership, w_out):
    n_seq = lax.axis_size("seq")
    groups = lax.axis_size("head")
    rank = lax.axis_index("seq")
    group = lax.axis_index("head")
    tok = queries.shape[0]
    heads = membership.shape[0]
    hd = queries.shape[1] // heads
    width = w_out.shape[1] // groups
    clusters = CL_DEV * n_seq
    cap = max(2, (2 * tok + clusters - 1) // clusters)
    rows = (CL_DEV * cap + 15) // 16 * 16
    near = n_seq * cap
    per_step = 2
    params = pltpu.CompilerParams(
        dimension_semantics=("arbitrary",),
        vmem_limit_bytes=63 * 1024 * 1024,
    )
    small = pltpu.CompilerParams(
        dimension_semantics=("arbitrary",),
        vmem_limit_bytes=(16 if n_seq <= 16 else 60) * 1024 * 1024,
    )
    exchange = functools.partial(
        lax.all_to_all, axis_name="seq", split_axis=0, concat_axis=0, tiled=True
    )
    swap = [(i, (i + 1) % groups) for i in range(groups)]

    mine = lax.dynamic_slice_in_dim(w_out, group * width, width, 1)
    other = lax.dynamic_slice_in_dim(w_out, (1 - group) * width, width, 1)
    other = lax.ppermute(other, "head", swap)

    matrix = pl.BlockSpec((tok, per_step * hd), lambda h: (0, h))
    line = pl.BlockSpec((per_step, 1, tok), lambda h: (h, 0, 0))
    column = pl.BlockSpec((tok, 128), lambda h: (0, 0))

    def slot_block(depth, count):
        return pl.BlockSpec((n_seq, count, rows, depth), lambda h: (0, h, 0, 0))

    def slot_array(depth):
        return jax.ShapeDtypeStruct((n_seq, heads, rows, depth), BF16)

    anywhere = pl.BlockSpec(memory_space=pl.ANY)
    in_vmem = pl.BlockSpec(memory_space=pltpu.VMEM)
    whole_params = pltpu.CompilerParams(vmem_limit_bytes=params.vmem_limit_bytes)
    send_kv, place = pl.pallas_call(
        functools.partial(pack_kv_kernel, rows, cap),
        grid=(heads // per_step,),
        in_specs=[line, matrix, matrix],
        out_specs=[slot_block(2 * hd, per_step), line],
        out_shape=[slot_array(2 * hd), jax.ShapeDtypeStruct((heads, 1, tok), jnp.int32)],
        scratch_shapes=[pltpu.VMEM((tok, tok), BF16)],
        compiler_params=params,
        name="pack_kv",
    )(membership.reshape(heads, 1, tok), keys, values)
    received_kv = exchange(send_kv)

    extra = (2 * heads * CL_DEV + 1 + 31) // 32 * 32
    all_rows = heads * rows + extra
    q_array = jax.ShapeDtypeStruct((n_seq, all_rows, hd), BF16)
    q_block = pl.BlockSpec((n_seq, per_step * rows, hd), lambda h: (0, h, 0))
    send_q, columns = pl.pallas_call(
        functools.partial(pack_q_kernel, rows),
        grid=(heads // per_step,),
        in_specs=[line, matrix],
        out_specs=[q_block, column],
        out_shape=[q_array, jax.ShapeDtypeStruct((tok, 128), jnp.int32)],
        compiler_params=params,
        name="pack_q",
    )(place, queries)

    send_q = pl.pallas_call(
        functools.partial(centers_kernel, cap),
        in_specs=[anywhere, anywhere],
        out_specs=anywhere,
        out_shape=q_array,
        scratch_shapes=[
            pltpu.VMEM((n_seq, heads, rows, 2 * hd), BF16),
            pltpu.VMEM((n_seq, extra, hd), BF16),
            pltpu.SemaphoreType.DMA((heads,)),
            pltpu.SemaphoreType.DMA,
        ],
        input_output_aliases={1: 0},
        compiler_params=whole_params,
        name="centers",
    )(received_kv, send_q)
    received_q = exchange(send_q)

    def near_block(count):
        return pl.BlockSpec((count, CL_DEV, near, 2 * hd), lambda h: (h, 0, 0, 0))

    near_pairs = pl.pallas_call(
        functools.partial(regroup_kernel, rows, cap),
        grid=(heads,),
        in_specs=[slot_block(2 * hd, 1)],
        out_specs=near_block(1),
        out_shape=jax.ShapeDtypeStruct((heads, CL_DEV, near, 2 * hd), BF16),
        scratch_shapes=[pltpu.VMEM((CL_DEV, near, n_seq * rows), BF16)],
        compiler_params=params,
        name="regroup",
    )(received_kv)

    answers = pl.pallas_call(
        functools.partial(attend_kernel, cap),
        in_specs=[pl.BlockSpec(memory_space=pltpu.SMEM), anywhere, anywhere],
        out_specs=anywhere,
        out_shape=slot_array(hd),
        scratch_shapes=[
            pltpu.VMEM((heads, clusters, 2 * hd), BF16),
            pltpu.VMEM((heads, clusters, 2 * hd), BF16),
            pltpu.VMEM((rows // 16, CL_DEV, n_seq * 16, hd), BF16),
            pltpu.VMEM((rows // 16, CL_DEV, n_seq * 16, hd), BF16),
            pltpu.VMEM((n_seq, all_rows, hd), BF16),
            pltpu.VMEM((heads, CL_DEV, near, 2 * hd), BF16),
            pltpu.VMEM((n_seq, heads, rows, hd), BF16),
            pltpu.SemaphoreType.DMA((2,)),
            pltpu.SemaphoreType.DMA((heads,)),
            pltpu.SemaphoreType.DMA((heads,)),
        ],
        compiler_params=whole_params,
        name="attend",
    )(rank.reshape(1), received_q, near_pairs)
    returned = exchange(answers)

    many = 3
    attended = pl.pallas_call(
        unpack_kernel,
        grid=(heads // many,),
        in_specs=[column, slot_block(hd, many)],
        out_specs=pl.BlockSpec((tok, many * hd), lambda h: (0, h)),
        out_shape=jax.ShapeDtypeStruct((tok, heads * hd), BF16),
        compiler_params=small,
        name="unpack",
    )(columns, returned)
    partner = lax.ppermute(attended, "head", swap)
    tail = pltpu.CompilerParams(vmem_limit_bytes=16 * 1024 * 1024)
    own_part, staged = pl.pallas_call(
        own_part_kernel,
        in_specs=[in_vmem] * 3,
        out_specs=[in_vmem] * 2,
        out_shape=[
            jax.ShapeDtypeStruct((tok, width), F32),
            jax.ShapeDtypeStruct(other.shape, BF16),
        ],
        compiler_params=tail,
        name="own_part",
    )(attended, mine, other)
    return pl.pallas_call(
        finish_kernel,
        in_specs=[in_vmem] * 3,
        out_specs=in_vmem,
        out_shape=jax.ShapeDtypeStruct((tok, width), BF16),
        compiler_params=tail,
        name="finish",
    )(own_part, partner, staged)


def solution(mesh):
    return jax.shard_map(
        per_device,
        mesh=mesh,
        in_specs=(
            P("seq", "head"),
            P("seq", "head"),
            P("seq", "head"),
            P("head", "seq", None),
            P("head", None),
        ),
        out_specs=P("seq", "head"),
        check_vma=False,
    )
```
